32 devices in a mesh: ctx: 8 (over z, y), fsdp: 4 (over x, core).
Axes of the slice: x: 2, y: 2, z: 4, core: 2. Of those that a mesh axis runs over, the one named last changes fastest.
Arguments:
- normed: bfloat16 [2, 4, 1024, 1024], P(None, 'fsdp', 'ctx'), may hold values from -6 to 6
- out_grad: bfloat16 [2, 4, 1024, 1024], P(None, 'fsdp', 'ctx'), may hold values from -6 to 6
- ids: int32 [2, 4, 1024], P(None, 'fsdp', 'ctx'), may hold values from 0 to 4, as said below
- mask: int32 [2, 4, 1024], P(None, 'fsdp', 'ctx'), may hold values 0 or 1
- proj_half: bfloat16 [512, 1024], P('fsdp'), may hold values from -0.1875 to 0.1875
- conv_filter: float32 [7, 1024], replicated, may hold values from -2.5 to 2.5
- gate_bias: float32 [6, 1024], replicated, may hold values from -6 to 6
Outputs:
- in_grad: bfloat16 [2, 4, 1024, 1024], P(None, 'fsdp', 'ctx')
- proj_grad: float32 [8, 512, 1024], P('ctx', 'fsdp')
- filter_grad: float32 [8, 7, 1024], P('ctx', None, 'fsdp')
- bias_grad: float32 [8, 6, 1024], P('ctx', None, 'fsdp')
The draws below stay inside these ranges and needn't reach their ends.
Inputs may be any that keep to these rules, and one draw needn't show every extreme that they name: Codes A=0, C=1, G=2, T=3, N=4. ids[1] is the reverse complement of ids[0] in its own coordinates: ids[1, b, p] = 3 - ids[0, b, 1023 - p] where that code is below 4, and 4 where it is 4. Every sequence holds at least one 4.
All inputs are finite; a program needn't handle non-finite values. No bound on the sum of `mask` on one device may be relied on, other than what follows from the above.
Results may differ from the reference program's by a relative error of at most 0.007.
Values may be sent and summed in bfloat16 or wider, within the bound.
A program may use at most 64 MiB of HBM per device.

```python
import math
import jax
import jax.numpy as jnp
from jax import lax

D = 1024
K = 7
ROWS = 128
SEQ = 1024
BATCH = 4
N_CTX = 8


def draw_ids(key, part):
    base_ids = jax.random.randint(jax.random.fold_in(key, 11), (BATCH, SEQ), 0, 4, dtype=jnp.int32)
    unknown = jax.random.randint(jax.random.fold_in(key, 12), (BATCH, SEQ), 0, 64, dtype=jnp.int32) == 0
    forced = jax.random.randint(jax.random.fold_in(key, 13), (BATCH, 1), 0, SEQ, dtype=jnp.int32)
    at_forced = lax.broadcasted_iota(jnp.int32, (BATCH, SEQ), 1) == forced
    forward = jnp.where(unknown | at_forced, 4, base_ids)
    reverse = jnp.flip(jnp.where(forward == 4, 4, 3 - forward), axis=1)
    return jnp.stack([forward, reverse], axis=0)


def touch_ends(entries, key, least, high):
    longest = entries.shape.index(max(entries.shape))
    spots = []
    for shift in (0, 1):
        where = [jax.random.randint(jax.random.fold_in(key, axis), (), 0, length) for axis, length in enumerate(entries.shape)]
        where[longest] = (where[longest] + shift) % entries.shape[longest]
        spots.append(tuple(where))
    return entries.at[spots[0]].set(least).at[spots[1]].set(high)


def steps_of(rng, shape, shards, least, largest):
    def one(axis_at, parts):
        steps = jax.random.uniform(jax.random.fold_in(jax.random.fold_in(rng, 6), axis_at), (parts,), jnp.float32, least / len(shards), largest / len(shards))
        return jnp.repeat(jnp.exp(steps), shape[axis_at] // parts).reshape((-1,) + (1,) * (len(shape) - axis_at - 1))

    factor_of = one(*shards[0])
    for cut in shards[1:]:
        factor_of = factor_of * one(*cut)
    return factor_of


def bell_draw(stream_key, extent, deviation, limit, cuts=(), kind=jnp.bfloat16):
    array = jax.random.normal(stream_key, extent, jnp.float32) * deviation
    if len(cuts) > 0:
        array = steps_of(stream_key, extent, cuts, -0.22, 0.18) * array
    return jnp.clip(array, min=-limit, max=limit).astype(kind)


def setup_inputs(seed: int = 0) -> dict:
    splits = jax.random.split(jax.random.key(seed), 8)
    return {
        "normed": bell_draw(splits[0], (2, BATCH, SEQ, D), 1.0, 6.0, ((1, 4), (2, 8))),
        "out_grad": bell_draw(splits[1], (2, BATCH, SEQ, D), 1.0, 6.0, ((1, 4), (2, 8))),
        "ids": draw_ids(jax.random.fold_in(splits[7], 71), 0),
        "mask": touch_ends((jax.random.randint(splits[3], (2, BATCH, SEQ), 0, 20) < 3).astype(jnp.int32), jax.random.fold_in(splits[3], 1), 0, 1),
        "proj_half": bell_draw(splits[4], (D // 2, D), D ** -0.5, 0.1875, ((0, 4),)),
        "conv_filter": bell_draw(splits[5], (K, D), 0.4, 2.5, (), jnp.float32),
        "gate_bias": bell_draw(splits[6], (6, D), 1.0, 6.0, (), jnp.float32),
    }


def reference(normed, out_grad, ids, mask, proj_half, conv_filter, gate_bias):
    weight_full = jnp.concatenate([proj_half, jnp.flip(proj_half, axis=(0, 1))], axis=0)
    half_width = D // 2
    scale = 1.0 / math.sqrt(2.0 * BATCH * ROWS)

    def one_sequence(totals, pieces):
        seq_in, seq_grad, seq_ids, seq_mask = pieces
        flat_in = seq_in.reshape(-1, D)
        values = jnp.dot(flat_in, weight_full, preferred_element_type=jnp.float32).astype(jnp.bfloat16).reshape(2, SEQ, D)
        extended = jnp.pad(values, ((0, 0), (K - 1, 0), (0, 0)))
        conv_out = jnp.zeros((2, SEQ, D), jnp.float32)
        for tap_index in range(K):
            start_row = K - 1 - tap_index
            conv_out = conv_out + conv_filter[tap_index] * extended[:, start_row:start_row + SEQ, :].astype(jnp.float32)
        mirrored = jnp.flip(values, axis=(0, 1, 2))
        tokens = jnp.where(seq_mask == 1, 5, seq_ids)
        gate = jax.nn.sigmoid(mirrored.astype(jnp.float32) + gate_bias[tokens])
        cotangent = seq_grad.astype(jnp.float32)
        conv_grad = cotangent * gate
        gate_pre = cotangent * conv_out * gate * (1.0 - gate)
        mirror_grad = gate_pre.astype(jnp.bfloat16)
        grad_ext = jnp.pad(conv_grad, ((0, 0), (0, K - 1), (0, 0)))
        value_grad = jnp.flip(mirror_grad, axis=(0, 1, 2)).astype(jnp.float32)
        for tap_index in range(K):
            value_grad = value_grad + conv_filter[tap_index] * grad_ext[:, tap_index:tap_index + SEQ, :]
        value_grad = value_grad.astype(jnp.bfloat16)
        flat_grad = value_grad.reshape(-1, D)
        in_grad = jnp.dot(flat_grad, weight_full.T, preferred_element_type=jnp.float32).astype(jnp.bfloat16).reshape(2, SEQ, D)
        blocks_in = seq_in.reshape(2, N_CTX, ROWS, D).astype(jnp.float32)
        blocks_grad = value_grad.reshape(2, N_CTX, ROWS, D).astype(jnp.float32)
        proj_part = jnp.einsum('scrd,scre->cde', blocks_in[..., :half_width], blocks_grad, precision=lax.Precision.HIGHEST)
        proj_part = proj_part + jnp.einsum('scrd,scre->cde', jnp.flip(blocks_in[..., half_width:], axis=3), jnp.flip(blocks_grad, axis=3), precision=lax.Precision.HIGHEST)
        filter_terms = []
        for tap_index in range(K):
            start_row = K - 1 - tap_index
            product = conv_grad * extended[:, start_row:start_row + SEQ, :].astype(jnp.float32)
            filter_terms.append(lax.optimization_barrier(jnp.sum(product.reshape(2, N_CTX, ROWS, D), axis=(0, 2))))
        filter_part = jnp.stack(filter_terms, axis=1)
        classes = jnp.arange(6, dtype=jnp.int32)
        one_hot = (tokens[..., None] == classes).astype(jnp.float32)
        bias_part = jnp.einsum('scrt,scrd->ctd', one_hot.reshape(2, N_CTX, ROWS, 6), gate_pre.reshape(2, N_CTX, ROWS, D), precision=lax.Precision.HIGHEST)
        totals = (totals[0] + proj_part, totals[1] + filter_part, totals[2] + bias_part)
        return (totals, in_grad)
    start_totals = (jnp.zeros((N_CTX, D // 2, D), jnp.float32), jnp.zeros((N_CTX, K, D), jnp.float32), jnp.zeros((N_CTX, 6, D), jnp.float32))
    pieces = (jnp.moveaxis(normed, 1, 0), jnp.moveaxis(out_grad, 1, 0), jnp.moveaxis(ids, 1, 0), jnp.moveaxis(mask, 1, 0))
    totals, grads_in = lax.scan(one_sequence, start_totals, pieces)
    in_grad = jnp.moveaxis(grads_in, 0, 1)
    return (in_grad, totals[0] * scale, totals[1] * scale, totals[2] * scale)
```

```python
import functools
import math

import jax
import jax.numpy as jnp
from jax import lax
from jax.experimental import pallas as pl
from jax.experimental.pallas import tpu as pltpu
from jax.sharding import PartitionSpec as P

MESH = pl.DeviceIdType.MESH
BF = jnp.bfloat16
F32 = jnp.float32
PAD = 8


def mm(a, b):
    return jnp.dot(a, b, preferred_element_type=F32)


def mm_nt(a, b):
    return lax.dot_general(a, b, (((1,), (1,)), ((), ())), preferred_element_type=F32)


def anti(size):
    row = lax.broadcasted_iota(jnp.int32, (size, size), 0)
    col = lax.broadcasted_iota(jnp.int32, (size, size), 1)
    return jnp.where(row + col == size - 1, 1.0, 0.0).astype(BF)


def eye(size):
    row = lax.broadcasted_iota(jnp.int32, (size, size), 0)
    col = lax.broadcasted_iota(jnp.int32, (size, size), 1)
    return jnp.where(row == col, 1.0, 0.0).astype(BF)


def split3(x):
    hi = x.astype(BF)
    rest = x - hi.astype(F32)
    mid = rest.astype(BF)
    low = (rest - mid.astype(F32)).astype(BF)
    return hi, mid, low


def flip_f32(x, j):
    hi, mid, low = split3(x)
    return (mm(hi, j) + mm(mid, j)) + mm(low, j)


def kernel(
    n, nf, taps, scale,
    n_ref, g_ref, ids_ref, mask_ref, proj_ref, filt_ref, bias_ref,
    in_out, proj_out, filt_out, bias_out,
    m_s, m_r, g1s, g1r, vgs, vgr, vg0, hs, hr, toks, tokr, w, v0, v1, cg0s, cg1s,
    gh0, gh1, oh, oht, gb, ft, fb, s0, s1, sr, at, pf, cs, cr, xs, xr,
    m_sem, g_sem, vg_sem, h_sem, t_sem, w_sem, wf_sem, s0_sem, s1_sem, c_sem, x_sem,
):
    rows, width = m_s.shape
    nc, _, cw = g1s.shape
    nx = nf // 2
    half = width // 2
    c = lax.axis_index("ctx")
    f = lax.axis_index("fsdp")
    core, chip = lax.rem(f, 2), f // 2
    sib = chip * 2 + 1 - core
    partner = n - 1 - c
    up, down = lax.rem(c + 1, n), lax.rem(c + n - 1, n)
    t_prev = lax.rem(2 * n - 2 - c, n)
    t_next = lax.rem(n - c, n)

    def rdma(src, dst, sems, cc, ff):
        return pltpu.make_async_remote_copy(
            src_ref=src, dst_ref=dst, send_sem=sems.at[0], recv_sem=sems.at[1],
            device_id=(cc, ff), device_id_type=MESH,
        )

    barrier = pltpu.get_barrier_semaphore()

    def greet(cc, ff):
        pl.semaphore_signal(barrier, inc=1, device_id=(cc, ff), device_id_type=MESH)

    for t in range(nf):
        greet(partner, lax.rem(f + t, nf))
    for t in range(1, nf):
        greet(c, lax.rem(f + t, nf))
    greet(up, f)
    greet(down, f)
    for target in (t_prev, t_next):
        @pl.when(target != c)
        def _():
            greet(target, f)

    jr = anti(rows)
    jc = anti(cw)

    def flip_cols(x):
        parts = [mm(x[:, q * cw : (q + 1) * cw], jc).astype(BF) for q in reversed(range(nc))]
        return jnp.concatenate(parts, axis=1)

    def pack(x):
        return jnp.concatenate([x[:, :half], x[:, half:]], axis=0).astype(BF)

    m_s[...] = flip_cols(mm(jr, n_ref[1]).astype(BF))
    toks[0:2, :] = jnp.where(mask_ref[...] == 1, 5, ids_ref[...])
    hs[0] = pack(n_ref[0, rows - 16 :, :].astype(F32)[16 - PAD :])
    hs[1] = pack(m_s[0:16, :].astype(F32)[:PAD])
    hs[2] = pack(g_ref[0, 0:16, :].astype(F32)[:PAD])
    hs[3] = pack(flip_cols(mm(jr, g_ref[1]).astype(BF)).astype(F32)[rows - PAD :])
    same_prev, same_next = t_prev == c, t_next == c
    pl.semaphore_wait(
        barrier,
        2 * nf + 1 + jnp.where(same_prev, 0, 1) + jnp.where(same_next, 0, 1),
    )

    m_copy = rdma(m_s, m_r, m_sem, partner, f)
    m_copy.start()
    w_far = [
        rdma(proj_ref, w.at[f], w_sem.at[t], c, lax.rem(chip + t, nx) * 2 + core)
        for t in range(1, nx)
    ]
    w_near = rdma(proj_ref, w.at[f], w_sem.at[0], c, sib)
    for copy in w_far:
        copy.start()
    w_near.start()
    h_up = rdma(hs.at[0], hr.at[0], h_sem.at[0], up, f)
    h_down = rdma(hs.at[2], hr.at[2], h_sem.at[2], down, f)
    h_prev = rdma(hs.at[1], hr.at[1], h_sem.at[1], t_prev, f)
    h_next = rdma(hs.at[3], hr.at[3], h_sem.at[3], t_next, f)
    k_pair = rdma(toks, tokr.at[0], t_sem.at[0], partner, f)
    k_down = rdma(toks, tokr.at[1], t_sem.at[1], down, f)
    k_next = rdma(toks, tokr.at[2], t_sem.at[2], t_next, f)
    for copy in (h_up, h_down, k_pair, k_down):
        copy.start()

    @pl.when(same_prev)
    def _():
        hr[1] = hs[1]

    @pl.when(jnp.logical_not(same_prev))
    def _():
        h_prev.start()

    @pl.when(same_next)
    def _():
        hr[3] = hs[3]
        tokr[2] = toks[...]

    @pl.when(jnp.logical_not(same_next))
    def _():
        h_next.start()
        k_next.start()

    def order(j):
        return jnp.where(lax.rem(j, 2) == 0, j // 2, nc - 1 - j // 2)

    def order_py(j):
        return j // 2 if j % 2 == 0 else nc - 1 - j // 2

    g_copies = []
    for j in range(nc):
        q = order_py(j)
        src = g_ref[1, :, (nc - 1 - q) * cw : (nc - q) * cw]
        g1s[q] = mm(mm(jr, src).astype(BF), jc).astype(BF)
        g_copies.append(rdma(g1s.at[q], g1r.at[q], g_sem.at[q], partner, f))
        g_copies[-1].start()

    fb[...] = jnp.zeros_like(fb)
    fb[0, 0:taps, :] = filt_ref[...]
    fb[1, 0 : bias_ref.shape[0], :] = bias_ref[...]
    for q in range(nc):
        cols = slice(q * cw, (q + 1) * cw)
        ft[0, q] = fb[0, :, cols]
        ft[1, nc - 1 - q] = flip_f32(fb[0, :, cols], jc)
        for strand, at_q in ((0, q), (1, nc - 1 - q)):
            table = fb[1, :, cols] if strand == 0 else flip_f32(fb[1, :, cols], jc)
            hi, mid, _ = split3(table)
            gb[strand, at_q] = jnp.concatenate([hi.astype(F32), mid.astype(F32)], axis=0).astype(BF)
    both = [
        n_ref[0, :, :half],
        n_ref[1, :, :half],
        flip_cols(n_ref[0])[:, :half],
        m_s[:, :half],
    ]
    both[3] = mm(jr, both[3]).astype(BF)
    for i, part in enumerate(both):
        at[:, i * rows : (i + 1) * rows] = part.astype(F32).T.astype(BF)

    w[f] = proj_ref[...]
    w_pass = []
    for t in range(1, nx):
        w_far[t - 1].wait_recv()
        src_f = lax.rem(chip + nx - t, nx) * 2 + core
        w_pass.append(rdma(w.at[src_f], w.at[src_f], wf_sem.at[t - 1], c, sib))
        w_pass[-1].start()
    w_near.wait_recv()
    for copy in w_pass:
        copy.wait_recv()
    for r in range(nf):
        w[2 * nf - 1 - r] = flip_cols(mm(jr, w[r]).astype(BF))

    h_up.wait_recv()
    h_down.wait_recv()
    k_pair.wait_recv()
    k_down.wait_recv()

    @pl.when(jnp.logical_not(same_prev))
    def _():
        h_prev.wait_recv()

    @pl.when(jnp.logical_not(same_next))
    def _():
        h_next.wait_recv()
        k_next.wait_recv()

    def unpack(x):
        x = x.astype(F32)
        return jnp.concatenate([x[:PAD], x[PAD:]], axis=1)

    first, last = c == 0, c == n - 1
    nh0 = jnp.where(first, 0.0, unpack(hr[0]))
    nh1 = jnp.where(last, 0.0, unpack(hr[1]))
    rim = jnp.concatenate([nh0, nh1], axis=0).astype(BF)
    gt0 = jnp.where(last, 0.0, unpack(hr[2]))
    gt1 = jnp.where(first, 0.0, unpack(hr[3]))
    classes = lax.rem(lax.broadcasted_iota(jnp.int32, (16, rows), 0), 8)
    sources = (toks[0:1, :], tokr[1, 0:1, :], tokr[0, 1:2, :], tokr[2, 1:2, :])
    for i, row in enumerate(sources):
        hot = jnp.where(classes == row, 1.0, 0.0).astype(BF)
        turn = eye(rows) if i < 2 else jr
        oh[i] = mm_nt(turn, hot).astype(BF)
        oht[i] = mm(hot, turn).astype(BF)
    for q in range(nc):
        cols = slice(q * cw, (q + 1) * cw)
        gh0[q] = gt0[:, cols]
        gh1[q] = gt1[:, cols]
        wq = w[:, :, cols].reshape(width, cw)
        v0[q, PAD:, :] = mm(n_ref[0], wq).astype(BF).astype(F32)
        edge = mm(rim, wq).astype(BF).astype(F32)
        v0[q, 0:PAD, :] = edge[:PAD]
        v1[q, rows:, :] = edge[PAD:]
    m_copy.wait_recv()
    for q in range(nc):
        wq = w[:, :, q * cw : (q + 1) * cw].reshape(width, cw)
        v1[q, 0:rows, :] = mm(m_r[...], wq).astype(BF).astype(F32)

    def column_step(j, carry):
        q = order(j)
        back = nc - 1 - q
        rdma(g1s.at[q], g1r.at[q], g_sem.at[q], partner, f).wait_recv()
        off = pl.multiple_of(q * cw, cw)
        g0 = jnp.concatenate([g_ref[0, :, pl.ds(off, cw)].astype(F32), gh0[q]], axis=0)
        g1 = jnp.concatenate([gh1[q], g1r[q].astype(F32)], axis=0)
        b0 = jnp.concatenate([mm(oh[0], gb[0, q]), mm(oh[1], gb[0, q])[:PAD]], axis=0)
        b1 = jnp.concatenate([mm(oh[3], gb[1, q])[rows - PAD :], mm(oh[2], gb[1, q])], axis=0)
        gate0 = jax.nn.sigmoid(v1[q] + b0)
        gate1 = jax.nn.sigmoid(v0[q] + b1)
        cg0s[...] = g0 * gate0
        cg1s[...] = g1 * gate1
        cg0, cg1 = cg0s[0:rows, :], cg1s[PAD:, :]
        conv0 = jnp.zeros((rows, cw), F32)
        conv1 = jnp.zeros((rows, cw), F32)
        for k in range(taps):
            a0 = v0[q, PAD - k : PAD - k + rows, :]
            a1 = v1[q, k : k + rows, :]
            conv0 = conv0 + ft[0, q, k : k + 1, :] * a0
            conv1 = conv1 + ft[1, q, k : k + 1, :] * a1
            s0[q, k : k + 1, :] = jnp.sum(cg0 * a0, axis=0, keepdims=True) * scale
            s1[back, k : k + 1, :] = jnp.sum(cg1 * a1, axis=0, keepdims=True) * scale
        s0[q, taps:8, :] = jnp.zeros((8 - taps, cw), F32)
        s1[back, taps:8, :] = jnp.zeros((8 - taps, cw), F32)
        gp0 = cg0 * conv0 * (1.0 - gate0[:rows])
        gp1 = cg1 * conv1 * (1.0 - gate1[PAD:])
        for store, at_q, hot, gp in ((s0, q, oht[0], gp0), (s1, back, oht[2], gp1)):
            hi, mid, _ = split3(gp)
            store[at_q, 8:16, :] = (mm(hot, hi) + mm(hot, mid))[:8] * scale
        s1[back] = flip_f32(s1[back], jc)
        vga = gp1.astype(BF).astype(F32)
        vgb = gp0.astype(BF).astype(F32)
        for k in range(taps):
            vga = vga + ft[0, q, k : k + 1, :] * cg0s[k : k + rows, :]
            vgb = vgb + ft[1, q, k : k + 1, :] * cg1s[PAD - k : PAD - k + rows, :]
        vg0[q] = vga.astype(BF)
        vgs[back] = mm(mm(jr, vgb.astype(BF)).astype(BF), jc).astype(BF)
        rdma(vgs.at[back], vgr.at[back], vg_sem.at[back], partner, f).start()
        return carry

    lax.fori_loop(0, nc, column_step, 0)

    small = []
    for t in range(nf):
        other = lax.rem(f + t, nf)
        small.append(rdma(s1.at[other], sr.at[1, t], s1_sem.at[t], partner, other))
        if t > 0:
            small.append(rdma(s0.at[other], sr.at[0, t], s0_sem.at[t], c, other))
    for copy in small:
        copy.start()

    def vg_wait(q):
        rdma(vgs.at[q], vgr.at[q], vg_sem.at[q], partner, f).wait_recv()

    def weight_part(p):
        lo, hi = p, nc - 1 - p
        vg_wait(hi)
        vg_wait(lo)
        for i, (a, b) in enumerate(((lo, hi), (hi, lo))):
            right = jnp.concatenate(
                [vg0[a], vgr[a], mm(vg0[b], jc).astype(BF), mm(vgr[b], jc).astype(BF)], axis=0
            )
            pf[p, i] = (mm(at[...], right) * scale).reshape(nf, half // nf, cw)
            for x in range(nx):
                cs[p, i * nx + x] = pf[p, i, 2 * x + 1 - core].astype(BF)
        copy = rdma(cs.at[p], cr.at[p], c_sem.at[p], c, sib)
        copy.start()
        return copy

    def weight_pass(p, copy):
        copy.wait_recv()
        out = []
        for t in range(1, nx):
            xt = lax.rem(chip + t, nx)
            for i in range(2):
                xs[p, t - 1, i] = (pf[p, i, 2 * xt + core] + cr[p, i * nx + xt].astype(F32)).astype(BF)
            out.append(rdma(xs.at[p, t - 1], xr.at[p, t - 1], x_sem.at[p, t - 1], c, 2 * xt + core))
            out[-1].start()
        return out

    def weight_end(p, copies):
        for copy in copies:
            copy.wait_recv()
        for i, q in enumerate((p, nc - 1 - p)):
            total = pf[p, i, f] + cr[p, i * nx + chip].astype(F32)
            for t in range(1, nx):
                total = total + xr[p, t - 1, i].astype(F32)
            proj_out[0, :, q * cw : (q + 1) * cw] = total

    def grad_in(strand, blocks):
        full = jnp.concatenate([blocks[q] for q in range(nc)], axis=1)
        for r in range(nf):
            wr = w[2 * r : 2 * r + 2].reshape(2 * w.shape[1], width)
            in_out[strand, :, r * wr.shape[0] : (r + 1) * wr.shape[0]] = mm_nt(full, wr).astype(BF)

    cores, crosses = [], []
    for p in range(nc // 2):
        cores.append(weight_part(p))
        if p == 0:
            grad_in(0, vg0)
        if p == nc // 2 - 1:
            grad_in(1, vgr)
        crosses.append(weight_pass(p, cores[p]))

    for copy in small:
        copy.wait_recv()
    total = s0[f] + sr[1, 0]
    for t in range(1, nf):
        total = total + sr[0, t] + sr[1, t]
    filt_out[0] = total[0:taps, :]
    bias_out[0] = total[8 : 8 + bias_out.shape[1], :]
    for p in range(nc // 2):
        weight_end(p, crosses[p])

    m_copy.wait_send()
    for copy in w_far + [w_near] + w_pass + [h_up, h_down, k_pair, k_down] + g_copies + small + cores:
        copy.wait_send()
    for copies in crosses:
        for copy in copies:
            copy.wait_send()
    for q in range(nc):
        rdma(vgs.at[q], vgr.at[q], vg_sem.at[q], partner, f).wait_send()

    @pl.when(jnp.logical_not(same_prev))
    def _():
        h_prev.wait_send()

    @pl.when(jnp.logical_not(same_next))
    def _():
        h_next.wait_send()
        k_next.wait_send()


def shards(n, nf, normed, out_grad, ids, mask, proj_half, conv_filter, gate_bias):
    _, seq_local, rows, width = normed.shape
    assert seq_local == 1
    taps, kinds = conv_filter.shape[0], gate_bias.shape[0]
    nc, cw, nx = nf, width // nf, nf // 2
    share = proj_half.shape[0]
    ext = rows + PAD
    scale = 1.0 / math.sqrt(2.0 * seq_local * nf * rows)
    vm = pltpu.VMEM
    dma = pltpu.SemaphoreType.DMA
    scratch = [
        vm((rows, width), BF), vm((rows, width), BF),
        vm((nc, rows, cw), BF), vm((nc, rows, cw), BF),
        vm((nc, rows, cw), BF), vm((nc, rows, cw), BF), vm((nc, rows, cw), BF),
        vm((4, 2 * PAD, width // 2), BF), vm((4, 2 * PAD, width // 2), BF),
        vm((8, rows), jnp.int32), vm((3, 8, rows), jnp.int32),
        vm((2 * nf, share, width), BF),
        vm((nc, ext, cw), F32), vm((nc, ext, cw), F32),
        vm((ext, cw), F32), vm((ext, cw), F32),
        vm((nc, PAD, cw), F32), vm((nc, PAD, cw), F32),
        vm((4, rows, 16), BF), vm((4, 16, rows), BF),
        vm((2, nc, 16, cw), BF), vm((2, nc, 8, cw), F32), vm((2, 8, width), F32),
        vm((nf, 16, cw), F32), vm((nf, 16, cw), F32), vm((2, nf, 16, cw), F32),
        vm((width // 2, 4 * rows), BF),
        vm((nc // 2, 2, nf, share, cw), F32),
        vm((nc // 2, 2 * nx, share, cw), BF), vm((nc // 2, 2 * nx, share, cw), BF),
        vm((nc // 2, nx - 1, 2, share, cw), BF), vm((nc // 2, nx - 1, 2, share, cw), BF),
        dma((2,)), dma((nc, 2)), dma((nc, 2)), dma((4, 2)), dma((3, 2)), dma((nx, 2)),
        dma((nx - 1, 2)), dma((nf, 2)), dma((nf, 2)), dma((nc // 2, 2)), dma((nc // 2, nx - 1, 2)),
    ]
    in_grad, proj, filt, bias = pl.pallas_call(
        functools.partial(kernel, n, nf, taps, scale),
        out_shape=(
            jax.ShapeDtypeStruct((2, rows, width), BF),
            jax.ShapeDtypeStruct((1, share, width), F32),
            jax.ShapeDtypeStruct((1, taps, cw), F32),
            jax.ShapeDtypeStruct((1, kinds, cw), F32),
        ),
        in_specs=[pl.BlockSpec(memory_space=pltpu.VMEM)] * 7,
        out_specs=[pl.BlockSpec(memory_space=pltpu.VMEM)] * 4,
        scratch_shapes=scratch,
        compiler_params=pltpu.CompilerParams(
            collective_id=0, has_side_effects=True, vmem_limit_bytes=48 * 1024 * 1024
        ),
    )(
        normed.reshape(2, rows, width),
        out_grad.reshape(2, rows, width),
        ids.reshape(2, rows),
        mask.reshape(2, rows),
        proj_half,
        conv_filter,
        gate_bias,
    )
    return in_grad.reshape(normed.shape), proj, filt, bias


def solution(mesh):
    placed = (
        P(None, "fsdp", "ctx", None),
        P(None, "fsdp", "ctx", None),
        P(None, "fsdp", "ctx"),
        P(None, "fsdp", "ctx"),
        P("fsdp", None),
        P(),
        P(),
    )
    return jax.shard_map(
        functools.partial(shards, mesh.shape["ctx"], mesh.shape["fsdp"]),
        mesh=mesh,
        in_specs=placed,
        out_specs=(
            P(None, "fsdp", "ctx", None),
            P("ctx", "fsdp", None),
            P("ctx", None, "fsdp"),
            P("ctx", None, "fsdp"),
        ),
        check_vma=False,
    )
```

```python
import functools
import math

import jax
import jax.numpy as jnp
from jax import lax
from jax.experimental import pallas as pl
from jax.experimental.pallas import tpu as pltpu
from jax.sharding import PartitionSpec as P

MESH = pl.DeviceIdType.MESH
BF = jnp.bfloat16
F32 = jnp.float32
PAD = 8


def mm(a, b):
    return jnp.dot(a, b, preferred_element_type=F32)


def mm_nt(a, b):
    return lax.dot_general(a, b, (((1,), (1,)), ((), ())), preferred_element_type=F32)


def anti(size):
    row = lax.broadcasted_iota(jnp.int32, (size, size), 0)
    col = lax.broadcasted_iota(jnp.int32, (size, size), 1)
    return jnp.where(row + col == size - 1, 1.0, 0.0).astype(BF)


def eye(size):
    row = lax.broadcasted_iota(jnp.int32, (size, size), 0)
    col = lax.broadcasted_iota(jnp.int32, (size, size), 1)
    return jnp.where(row == col, 1.0, 0.0).astype(BF)


def split3(x):
    hi = x.astype(BF)
    rest = x - hi.astype(F32)
    mid = rest.astype(BF)
    low = (rest - mid.astype(F32)).astype(BF)
    return hi, mid, low


def flip_f32(x, j):
    hi, mid, low = split3(x)
    return (mm(hi, j) + mm(mid, j)) + mm(low, j)


def kernel(
    n, nf, taps, scale,
    n_hbm, g_hbm, ids_hbm, mask_hbm, proj_ref, filt_hbm, bias_hbm,
    in_out, proj_out, filt_out, bias_out,
    n_ref, g_ref, ids_ref, mask_ref, filt_ref, bias_ref, s1t, s1r,
    m_s, m_r, g1s, g1r, vgs, vgr, vg0, hs, hr, toks, tokr, w, v0, v1, cg0s, cg1s,
    gh0, gh1, oh, oht, gb, ft, fb, s0, s1, sr, at, pf, cs, cr, xs, xr,
    in_sem, s1t_sem, m_sem, g_sem, vg_sem, h_sem, t_sem, w_sem, wf_sem, s0_sem, s1_sem, c_sem, x_sem,
):
    rows, width = m_s.shape
    nc, _, cw = g1s.shape
    nx = nf // 2
    half = width // 2
    c = lax.axis_index("ctx")
    f = lax.axis_index("fsdp")
    core, chip = lax.rem(f, 2), f // 2
    sib = chip * 2 + 1 - core
    partner = n - 1 - c
    up, down = lax.rem(c + 1, n), lax.rem(c + n - 1, n)
    t_prev = lax.rem(2 * n - 2 - c, n)
    t_next = lax.rem(n - c, n)

    def rdma(src, dst, sems, cc, ff):
        return pltpu.make_async_remote_copy(
            src_ref=src, dst_ref=dst, send_sem=sems.at[0], recv_sem=sems.at[1],
            device_id=(cc, ff), device_id_type=MESH,
        )

    loads = [
        pltpu.make_async_copy(src, dst, in_sem.at[i])
        for i, (src, dst) in enumerate(
            (
                (n_hbm.at[1], n_ref.at[1]),
                (g_hbm.at[1], g_ref.at[1]),
                (ids_hbm, ids_ref),
                (mask_hbm, mask_ref),
                (n_hbm.at[0], n_ref.at[0]),
                (g_hbm.at[0], g_ref.at[0]),
                (filt_hbm, filt_ref),
                (bias_hbm, bias_ref),
                (proj_ref, w.at[f]),
            )
        )
    ]
    for load in loads:
        load.start()
    barrier = pltpu.get_barrier_semaphore()

    def greet(cc, ff):
        pl.semaphore_signal(barrier, inc=1, device_id=(cc, ff), device_id_type=MESH)

    for t in range(nf):
        greet(partner, lax.rem(f + t, nf))
    for t in range(1, nf):
        greet(c, lax.rem(f + t, nf))
    greet(up, f)
    greet(down, f)
    for target in (t_prev, t_next):
        @pl.when(target != c)
        def _():
            greet(target, f)

    jr = anti(rows)
    jc = anti(cw)

    def flip_cols(x):
        parts = [mm(x[:, q * cw : (q + 1) * cw], jc).astype(BF) for q in reversed(range(nc))]
        return jnp.concatenate(parts, axis=1)

    def pack(x):
        return jnp.concatenate([x[:, :half], x[:, half:]], axis=0).astype(BF)

    loads[0].wait()
    m_s[...] = flip_cols(mm(jr, n_ref[1]).astype(BF))
    same_prev, same_next = t_prev == c, t_next == c
    pl.semaphore_wait(
        barrier,
        2 * nf + 1 + jnp.where(same_prev, 0, 1) + jnp.where(same_next, 0, 1),
    )

    m_copy = rdma(m_s, m_r, m_sem, partner, f)
    m_copy.start()
    w_far = [
        rdma(proj_ref, w.at[f], w_sem.at[t], c, lax.rem(chip + t, nx) * 2 + core)
        for t in range(1, nx)
    ]
    w_near = rdma(proj_ref, w.at[f], w_sem.at[0], c, sib)
    for copy in w_far:
        copy.start()
    w_near.start()
    for load in loads[1:]:
        load.wait()
    for i in range(2):
        toks[i : i + 1, :] = jnp.where(mask_ref[i] == 1, 5, ids_ref[i])
    hs[0] = pack(n_ref[0, rows - 16 :, :].astype(F32)[16 - PAD :])
    hs[1] = pack(m_s[0:16, :].astype(F32)[:PAD])
    hs[2] = pack(g_ref[0, 0:16, :].astype(F32)[:PAD])
    hs[3] = pack(flip_cols(mm(anti(16), g_ref[1, 0:16, :]).astype(BF)).astype(F32)[16 - PAD :])
    h_up = rdma(hs.at[0], hr.at[0], h_sem.at[0], up, f)
    h_down = rdma(hs.at[2], hr.at[2], h_sem.at[2], down, f)
    h_prev = rdma(hs.at[1], hr.at[1], h_sem.at[1], t_prev, f)
    h_next = rdma(hs.at[3], hr.at[3], h_sem.at[3], t_next, f)
    k_pair = rdma(toks, tokr.at[0], t_sem.at[0], partner, f)
    k_down = rdma(toks, tokr.at[1], t_sem.at[1], down, f)
    k_next = rdma(toks, tokr.at[2], t_sem.at[2], t_next, f)
    for copy in (h_up, h_down, k_pair, k_down):
        copy.start()

    @pl.when(same_prev)
    def _():
        hr[1] = hs[1]

    @pl.when(jnp.logical_not(same_prev))
    def _():
        h_prev.start()

    @pl.when(same_next)
    def _():
        hr[3] = hs[3]
        tokr[2] = toks[...]

    @pl.when(jnp.logical_not(same_next))
    def _():
        h_next.start()
        k_next.start()

    def order(j):
        return jnp.where(lax.rem(j, 2) == 0, j // 2, nc - 1 - j // 2)

    def order_py(j):
        return j // 2 if j % 2 == 0 else nc - 1 - j // 2

    g_copies = []
    for j in range(nc):
        q = order_py(j)
        src = g_ref[1, :, (nc - 1 - q) * cw : (nc - q) * cw]
        g1s[q] = mm(mm(jr, src).astype(BF), jc).astype(BF)
        g_copies.append(rdma(g1s.at[q], g1r.at[q], g_sem.at[q], partner, f))
        g_copies[-1].start()

    fb[...] = jnp.zeros_like(fb)
    fb[0, 0:taps, :] = filt_ref[...]
    fb[1, 0 : bias_ref.shape[0], :] = bias_ref[...]
    for q in range(nc):
        cols = slice(q * cw, (q + 1) * cw)
        ft[0, q] = fb[0, :, cols]
        ft[1, nc - 1 - q] = flip_f32(fb[0, :, cols], jc)
        for strand, at_q in ((0, q), (1, nc - 1 - q)):
            table = fb[1, :, cols] if strand == 0 else flip_f32(fb[1, :, cols], jc)
            hi, mid, _ = split3(table)
            gb[strand, at_q] = jnp.concatenate([hi.astype(F32), mid.astype(F32)], axis=0).astype(BF)
    both = [
        n_ref[0, :, :half],
        n_ref[1, :, :half],
        flip_cols(n_ref[0])[:, :half],
        m_s[:, :half],
    ]
    both[3] = mm(jr, both[3]).astype(BF)
    for i, part in enumerate(both):
        at[:, i * rows : (i + 1) * rows] = part.astype(F32).T.astype(BF)

    w_pass = []
    for t in range(1, nx):
        w_far[t - 1].wait_recv()
        src_f = lax.rem(chip + nx - t, nx) * 2 + core
        w_pass.append(rdma(w.at[src_f], w.at[src_f], wf_sem.at[t - 1], c, sib))
        w_pass[-1].start()
    w_near.wait_recv()
    for copy in w_pass:
        copy.wait_recv()
    for r in range(nf):
        w[2 * nf - 1 - r] = flip_cols(mm(jr, w[r]).astype(BF))

    h_up.wait_recv()
    h_down.wait_recv()
    k_pair.wait_recv()
    k_down.wait_recv()

    @pl.when(jnp.logical_not(same_prev))
    def _():
        h_prev.wait_recv()

    @pl.when(jnp.logical_not(same_next))
    def _():
        h_next.wait_recv()
        k_next.wait_recv()

    def unpack(x):
        x = x.astype(F32)
        return jnp.concatenate([x[:PAD], x[PAD:]], axis=1)

    first, last = c == 0, c == n - 1
    nh0 = jnp.where(first, 0.0, unpack(hr[0]))
    nh1 = jnp.where(last, 0.0, unpack(hr[1]))
    rim = jnp.concatenate([nh0, nh1], axis=0).astype(BF)
    gt0 = jnp.where(last, 0.0, unpack(hr[2]))
    gt1 = jnp.where(first, 0.0, unpack(hr[3]))
    classes = lax.rem(lax.broadcasted_iota(jnp.int32, (16, rows), 0), 8)
    sources = (toks[0:1, :], tokr[1, 0:1, :], tokr[0, 1:2, :], tokr[2, 1:2, :])
    for i, row in enumerate(sources):
        hot = jnp.where(classes == row, 1.0, 0.0).astype(BF)
        turn = eye(rows) if i < 2 else jr
        oh[i] = mm_nt(turn, hot).astype(BF)
        oht[i] = mm(hot, turn).astype(BF)
    for q in range(nc):
        cols = slice(q * cw, (q + 1) * cw)
        gh0[q] = gt0[:, cols]
        gh1[q] = gt1[:, cols]
        wq = w[:, :, cols].reshape(width, cw)
        v0[q, PAD:, :] = mm(n_ref[0], wq).astype(BF).astype(F32)
        edge = mm(rim, wq).astype(BF).astype(F32)
        v0[q, 0:PAD, :] = edge[:PAD]
        v1[q, rows:, :] = edge[PAD:]
    m_copy.wait_recv()
    for q in range(nc):
        wq = w[:, :, q * cw : (q + 1) * cw].reshape(width, cw)
        v1[q, 0:rows, :] = mm(m_r[...], wq).astype(BF).astype(F32)

    def column_step(j, carry):
        q = order(j)
        back = nc - 1 - q
        rdma(g1s.at[q], g1r.at[q], g_sem.at[q], partner, f).wait_recv()
        off = pl.multiple_of(q * cw, cw)
        g0 = jnp.concatenate([g_ref[0, :, pl.ds(off, cw)].astype(F32), gh0[q]], axis=0)
        g1 = jnp.concatenate([gh1[q], g1r[q].astype(F32)], axis=0)
        b0 = jnp.concatenate([mm(oh[0], gb[0, q]), mm(oh[1], gb[0, q])[:PAD]], axis=0)
        b1 = jnp.concatenate([mm(oh[3], gb[1, q])[rows - PAD :], mm(oh[2], gb[1, q])], axis=0)
        gate0 = jax.nn.sigmoid(v1[q] + b0)
        gate1 = jax.nn.sigmoid(v0[q] + b1)
        cg0s[...] = g0 * gate0
        cg1s[...] = g1 * gate1
        cg0, cg1 = cg0s[0:rows, :], cg1s[PAD:, :]
        conv0 = jnp.zeros((rows, cw), F32)
        conv1 = jnp.zeros((rows, cw), F32)
        for k in range(taps):
            a0 = v0[q, PAD - k : PAD - k + rows, :]
            a1 = v1[q, k : k + rows, :]
            conv0 = conv0 + ft[0, q, k : k + 1, :] * a0
            conv1 = conv1 + ft[1, q, k : k + 1, :] * a1
            s0[q, k : k + 1, :] = jnp.sum(cg0 * a0, axis=0, keepdims=True) * scale
            s1[back, k : k + 1, :] = jnp.sum(cg1 * a1, axis=0, keepdims=True) * scale
        s0[q, taps:8, :] = jnp.zeros((8 - taps, cw), F32)
        s1[back, taps:8, :] = jnp.zeros((8 - taps, cw), F32)
        gp0 = cg0 * conv0 * (1.0 - gate0[:rows])
        gp1 = cg1 * conv1 * (1.0 - gate1[PAD:])
        for store, at_q, hot, gp in ((s0, q, oht[0], gp0), (s1, back, oht[2], gp1)):
            hi, mid, _ = split3(gp)
            store[at_q, 8:16, :] = (mm(hot, hi) + mm(hot, mid))[:8] * scale
        s1[back] = flip_f32(s1[back], jc)
        vga = gp1.astype(BF).astype(F32)
        vgb = gp0.astype(BF).astype(F32)
        for k in range(taps):
            vga = vga + ft[0, q, k : k + 1, :] * cg0s[k : k + rows, :]
            vgb = vgb + ft[1, q, k : k + 1, :] * cg1s[PAD - k : PAD - k + rows, :]
        vg0[q] = vga.astype(BF)
        vgs[back] = mm(mm(jr, vgb.astype(BF)).astype(BF), jc).astype(BF)
        rdma(vgs.at[back], vgr.at[back], vg_sem.at[back], partner, f).start()
        return carry

    lax.fori_loop(0, nc, column_step, 0)

    small = []
    for t in range(1, nf):
        other = lax.rem(f + t, nf)
        small.append(rdma(s1.at[other], sr.at[1, t], s1_sem.at[t], c, other))
        small.append(rdma(s0.at[other], sr.at[0, t], s0_sem.at[t], c, other))
    for copy in small:
        copy.start()

    def vg_wait(q):
        rdma(vgs.at[q], vgr.at[q], vg_sem.at[q], partner, f).wait_recv()

    def weight_part(p):
        lo, hi = p, nc - 1 - p
        vg_wait(hi)
        vg_wait(lo)
        for i, (a, b) in enumerate(((lo, hi), (hi, lo))):
            right = jnp.concatenate(
                [vg0[a], vgr[a], mm(vg0[b], jc).astype(BF), mm(vgr[b], jc).astype(BF)], axis=0
            )
            pf[p, i] = (mm(at[...], right) * scale).reshape(nf, half // nf, cw)
            for x in range(nx):
                cs[p, i * nx + x] = pf[p, i, 2 * x + 1 - core].astype(BF)
        copy = rdma(cs.at[p], cr.at[p], c_sem.at[p], c, sib)
        copy.start()
        return copy

    def weight_pass(p, copy):
        copy.wait_recv()
        out = []
        for t in range(1, nx):
            xt = lax.rem(chip + t, nx)
            for i in range(2):
                xs[p, t - 1, i] = (pf[p, i, 2 * xt + core] + cr[p, i * nx + xt].astype(F32)).astype(BF)
            out.append(rdma(xs.at[p, t - 1], xr.at[p, t - 1], x_sem.at[p, t - 1], c, 2 * xt + core))
            out[-1].start()
        return out

    def weight_end(p, copies):
        for copy in copies:
            copy.wait_recv()
        for i, q in enumerate((p, nc - 1 - p)):
            total = pf[p, i, f] + cr[p, i * nx + chip].astype(F32)
            for t in range(1, nx):
                total = total + xr[p, t - 1, i].astype(F32)
            proj_out[0, :, q * cw : (q + 1) * cw] = total

    def grad_in(strand, blocks):
        full = jnp.concatenate([blocks[q] for q in range(nc)], axis=1)
        for r in range(nf):
            wr = w[2 * r : 2 * r + 2].reshape(2 * w.shape[1], width)
            in_out[strand, :, r * wr.shape[0] : (r + 1) * wr.shape[0]] = mm_nt(full, wr).astype(BF)

    grad_in(0, vg0)
    for copy in small:
        copy.wait_recv()
    total, across = s0[f], s1[f]
    for t in range(1, nf):
        total = total + sr[0, t]
        across = across + sr[1, t]
    s1t[...] = across
    s1_copy = rdma(s1t, s1r, s1t_sem, partner, f)
    s1_copy.start()
    cores, crosses = [], []
    for p in range(nc // 2):
        cores.append(weight_part(p))
        if p == nc // 2 - 1:
            grad_in(1, vgr)
        crosses.append(weight_pass(p, cores[p]))

    s1_copy.wait_recv()
    total = total + s1r[...]
    filt_out[0] = total[0:taps, :]
    bias_out[0] = total[8 : 8 + bias_out.shape[1], :]
    for p in range(nc // 2):
        weight_end(p, crosses[p])

    m_copy.wait_send()
    s1_copy.wait_send()
    for copy in w_far + [w_near] + w_pass + [h_up, h_down, k_pair, k_down] + g_copies + small + cores:
        copy.wait_send()
    for copies in crosses:
        for copy in copies:
            copy.wait_send()
    for q in range(nc):
        rdma(vgs.at[q], vgr.at[q], vg_sem.at[q], partner, f).wait_send()

    @pl.when(jnp.logical_not(same_prev))
    def _():
        h_prev.wait_send()

    @pl.when(jnp.logical_not(same_next))
    def _():
        h_next.wait_send()
        k_next.wait_send()


def shards(n, nf, normed, out_grad, ids, mask, proj_half, conv_filter, gate_bias):
    _, seq_local, rows, width = normed.shape
    assert seq_local == 1
    taps, kinds = conv_filter.shape[0], gate_bias.shape[0]
    nc, cw, nx = nf, width // nf, nf // 2
    share = proj_half.shape[0]
    ext = rows + PAD
    scale = 1.0 / math.sqrt(2.0 * seq_local * nf * rows)
    vm = pltpu.VMEM
    dma = pltpu.SemaphoreType.DMA
    scratch = [
        vm((2, rows, width), BF), vm((2, rows, width), BF),
        vm((2, 1, rows), jnp.int32), vm((2, 1, rows), jnp.int32),
        vm((taps, width), F32), vm((kinds, width), F32),
        vm((16, cw), F32), vm((16, cw), F32),
        vm((rows, width), BF), vm((rows, width), BF),
        vm((nc, rows, cw), BF), vm((nc, rows, cw), BF),
        vm((nc, rows, cw), BF), vm((nc, rows, cw), BF), vm((nc, rows, cw), BF),
        vm((4, 2 * PAD, width // 2), BF), vm((4, 2 * PAD, width // 2), BF),
        vm((8, rows), jnp.int32), vm((3, 8, rows), jnp.int32),
        vm((2 * nf, share, width), BF),
        vm((nc, ext, cw), F32), vm((nc, ext, cw), F32),
        vm((ext, cw), F32), vm((ext, cw), F32),
        vm((nc, PAD, cw), F32), vm((nc, PAD, cw), F32),
        vm((4, rows, 16), BF), vm((4, 16, rows), BF),
        vm((2, nc, 16, cw), BF), vm((2, nc, 8, cw), F32), vm((2, 8, width), F32),
        vm((nf, 16, cw), F32), vm((nf, 16, cw), F32), vm((2, nf, 16, cw), F32),
        vm((width // 2, 4 * rows), BF),
        vm((nc // 2, 2, nf, share, cw), F32),
        vm((nc // 2, 2 * nx, share, cw), BF), vm((nc // 2, 2 * nx, share, cw), BF),
        vm((nc // 2, nx - 1, 2, share, cw), BF), vm((nc // 2, nx - 1, 2, share, cw), BF),
        dma((9,)), dma((2,)), dma((2,)), dma((nc, 2)), dma((nc, 2)), dma((4, 2)), dma((3, 2)), dma((nx, 2)),
        dma((nx - 1, 2)), dma((nf, 2)), dma((nf, 2)), dma((nc // 2, 2)), dma((nc // 2, nx - 1, 2)),
    ]
    in_grad, proj, filt, bias = pl.pallas_call(
        functools.partial(kernel, n, nf, taps, scale),
        out_shape=(
            jax.ShapeDtypeStruct((2, rows, width), BF),
            jax.ShapeDtypeStruct((1, share, width), F32),
            jax.ShapeDtypeStruct((1, taps, cw), F32),
            jax.ShapeDtypeStruct((1, kinds, cw), F32),
        ),
        in_specs=[pl.BlockSpec(memory_space=pltpu.HBM)] * 7,
        out_specs=[pl.BlockSpec(memory_space=pltpu.VMEM)] * 4,
        scratch_shapes=scratch,
        compiler_params=pltpu.CompilerParams(
            collective_id=0, has_side_effects=True, vmem_limit_bytes=56 * 1024 * 1024
        ),
    )(
        normed.reshape(2, rows, width),
        out_grad.reshape(2, rows, width),
        ids,
        mask,
        proj_half,
        conv_filter,
        gate_bias,
    )
    return in_grad.reshape(normed.shape), proj, filt, bias


def solution(mesh):
    placed = (
        P(None, "fsdp", "ctx", None),
        P(None, "fsdp", "ctx", None),
        P(None, "fsdp", "ctx"),
        P(None, "fsdp", "ctx"),
        P("fsdp", None),
        P(),
        P(),
    )
    return jax.shard_map(
        functools.partial(shards, mesh.shape["ctx"], mesh.shape["fsdp"]),
        mesh=mesh,
        in_specs=placed,
        out_specs=(
            P(None, "fsdp", "ctx", None),
            P("ctx", "fsdp", None),
            P("ctx", None, "fsdp"),
            P("ctx", None, "fsdp"),
        ),
        check_vma=False,
    )
```
